512 devices in a mesh: dp: 8 (over z_hi, core), seq: 64 (over z_lo, y, x).
Axes of the slice: x: 4, y: 8, z: 8 (z_hi: 4, z_lo: 2; z = z_hi * 2 + z_lo), core: 2. Of those that a mesh axis runs over, the one named last changes fastest.
Arguments:
- query_gate: bfloat16 [8, 16384, 256], P('dp', 'seq'), may hold values from -6 to 6
- key_gate: bfloat16 [8, 16384, 256], P('dp', 'seq'), may hold values from -6 to 6
- values_in: bfloat16 [8, 16384, 256], P('dp', 'seq'), may hold values from -6 to 6
- grad_out: bfloat16 [8, 16384, 256], P('dp', 'seq'), may hold values from -6 to 6
- long_filter: bfloat16 [16384, 256], P('seq'), may hold values from -6 to 6
Outputs:
- grad_query: bfloat16 [8, 16384, 256], P('dp', 'seq')
- grad_key: bfloat16 [8, 16384, 256], P('dp', 'seq')
- grad_value: bfloat16 [8, 16384, 256], P('dp', 'seq')
- grad_filter: float32 [16384, 256], P('seq')
The draws below stay inside these ranges and needn't reach their ends.
All inputs are finite; a program needn't handle non-finite values.
Results may differ from the reference program's by a relative error of at most 0.0049.
Values may be sent and summed in bfloat16 or wider, within the bound.
No kernel may reach another device: no remote copies, remote signals or barrier semaphores. Data moves between devices by JAX's collectives and lax.ppermute only.
A program may use at most 64 MiB of HBM per device.

```python
import math
import jax
import jax.numpy as jnp
from jax import lax

CH = 256
SEQ = 16384
NFFT = 32768
BATCH = 8


def block_scale(rng, dims, split, low, high):
    def one(axis_at, shards_of):
        draws = jax.random.uniform(jax.random.fold_in(jax.random.fold_in(rng, 6), axis_at), (shards_of,), jnp.float32, low / len(split), high / len(split))
        return jnp.repeat(jnp.exp(draws), dims[axis_at] // shards_of).reshape((-1,) + (1,) * (len(dims) - axis_at - 1))

    gain = one(*split[0])
    for cut in split[1:]:
        gain = gain * one(*cut)
    return gain


def gaussian(own_key, extent, deviation, limit, pieces=(), held_as=jnp.bfloat16):
    factor_of = block_scale(own_key, extent, pieces, -0.22, 0.18) if pieces else 1.0
    drawn = jax.random.normal(own_key, extent, jnp.float32) * deviation * factor_of
    return jnp.minimum(jnp.maximum(drawn, -limit), limit).astype(held_as)


def setup_inputs(seed: int = 0) -> dict:
    key_of = jax.random.split(jax.random.key(seed), 6)
    return {
        "query_gate": gaussian(key_of[0], (BATCH, SEQ, CH), 1.0, 6.0, ((0, 8), (1, 64))),
        "key_gate": gaussian(key_of[1], (BATCH, SEQ, CH), 1.0, 6.0, ((0, 8), (1, 64))),
        "values_in": gaussian(key_of[2], (BATCH, SEQ, CH), 1.0, 6.0, ((0, 8), (1, 64))),
        "grad_out": gaussian(key_of[3], (BATCH, SEQ, CH), 1.0, 6.0, ((0, 8), (1, 64))),
        "long_filter": gaussian(key_of[4], (SEQ, CH), 1.0, 6.0, ((0, 64),)),
    }


def reference(query_gate, key_gate, values_in, grad_out, long_filter):
    scaling = 1.0 / math.sqrt(SEQ)
    spec_filter = jnp.fft.fft(long_filter.astype(jnp.float32) * scaling, n=NFFT, axis=0)

    def one_sequence(items):
        query_one, key_one, value_one, grad_one = items
        mixed_in = (key_one.astype(jnp.float32) * value_one.astype(jnp.float32)).astype(jnp.bfloat16)
        gated_grad = (grad_one.astype(jnp.float32) * query_one.astype(jnp.float32)).astype(jnp.bfloat16)
        spec_mixed = jnp.fft.fft(mixed_in.astype(jnp.float32), n=NFFT, axis=0)
        spec_gated = jnp.fft.fft(gated_grad.astype(jnp.float32), n=NFFT, axis=0)
        conv_out = jnp.real(jnp.fft.ifft(spec_mixed * spec_filter, axis=0))[:SEQ]
        grad_mixed = jnp.real(jnp.fft.ifft(spec_gated * jnp.conj(spec_filter), axis=0))[:SEQ]
        filter_part = jnp.real(jnp.fft.ifft(spec_gated * jnp.conj(spec_mixed), axis=0))[:SEQ]
        grad_query = (grad_one.astype(jnp.float32) * conv_out).astype(jnp.bfloat16)
        grad_key = (grad_mixed * value_one.astype(jnp.float32)).astype(jnp.bfloat16)
        grad_value = (grad_mixed * key_one.astype(jnp.float32)).astype(jnp.bfloat16)
        return (grad_query, grad_key, grad_value, filter_part)
    grad_query, grad_key, grad_value, filter_parts = lax.map(one_sequence, (query_gate, key_gate, values_in, grad_out))
    grad_filter = lax.optimization_barrier(jnp.sum(filter_parts, axis=0)) * scaling
    return (grad_query, grad_key, grad_value, grad_filter)
```

```python
import math

import jax
import jax.numpy as jnp
import numpy as np
from jax import lax
from jax.experimental import pallas as pl
from jax.experimental.pallas import tpu as pltpu
from jax.sharding import Mesh, PartitionSpec as P

HI, CORE, LO, Y, X = "hi", "core", "lo", "y", "x"
SIZES = (4, 2, 2, 8, 4)
SEQ_AXES = (LO, Y, X)
GROUP = (HI, LO, Y, X)
BLOCKS = 64
WIDTH = 256
ROWS = 64
LENGTH = 2 * BLOCKS * WIDTH


def split_bf16(array):
    high = array.astype(jnp.bfloat16)
    low = (array - high.astype(np.float32)).astype(jnp.bfloat16)
    return high, low


def tables():
    freq = np.arange(ROWS)[:, None] + 0.5
    block = np.arange(BLOCKS)[None, :]
    place = np.arange(WIDTH)
    angle = 2.0 * math.pi * freq * block / (2 * BLOCKS)
    enter = np.concatenate([np.cos(angle), -np.sin(angle)], axis=0).astype(np.float32)
    scale = 2.0 / LENGTH / math.sqrt(BLOCKS * WIDTH)
    leave = (scale * np.concatenate([np.cos(angle.T), -np.sin(angle.T)], axis=1)).astype(np.float32)
    turn = 2.0 * math.pi * freq * place[None, :] / LENGTH
    angle = 2.0 * math.pi * (place[:, None] * place[None, :] % WIDTH) / WIDTH
    cos_high, cos_low = split_bf16(np.cos(angle).astype(np.float32))
    sin_high, sin_low = split_bf16(np.sin(angle).astype(np.float32))
    return (
        np.concatenate(split_bf16(enter), axis=1),
        np.cos(turn).astype(np.float32),
        np.sin(turn).astype(np.float32),
        np.stack([cos_high, cos_low, sin_high, sin_low]),
        np.stack(split_bf16(leave)),
    )


def dot(left, right):
    return jnp.dot(left, right, preferred_element_type=jnp.float32)


def halves(array):
    high = array.astype(jnp.bfloat16)
    return high, (array - high.astype(jnp.float32)).astype(jnp.bfloat16)


def times_table(high, low, table_ref, at):
    return dot(high, table_ref[at]) + dot(low, table_ref[at]) + dot(high, table_ref[at + 1])


def convolve_kernel(x_ref, enter_ref, cos_ref, sin_ref, table_ref, leave_ref, out_ref):
    sequences = x_ref.shape[0] // BLOCKS
    turn_cos, turn_sin = cos_ref[...], sin_ref[...]
    signals = []
    for one in range(sequences):
        rows = slice(one * BLOCKS, (one + 1) * BLOCKS)
        signals += [x_ref[rows, :WIDTH], x_ref[rows, WIDTH : 2 * WIDTH]]
    signals.append(x_ref[:BLOCKS, 2 * WIDTH :])
    real_parts, imag_parts = [], []
    for signal in signals:
        first = dot(enter_ref[...], jnp.concatenate([signal, signal], axis=0))
        real, imag = first[:ROWS], first[ROWS:]
        real_parts.append(real * turn_cos + imag * turn_sin)
        imag_parts.append(imag * turn_cos - real * turn_sin)
    high, low = halves(jnp.concatenate(real_parts + imag_parts, axis=0))
    by_cos = times_table(high, low, table_ref, 0)
    by_sin = times_table(high, low, table_ref, 2)
    count = len(signals)
    half = count * ROWS
    spec_real = by_cos[:half] + by_sin[half:]
    spec_imag = by_cos[half:] - by_sin[:half]
    spectra = [
        (spec_real[i * ROWS : (i + 1) * ROWS], spec_imag[i * ROWS : (i + 1) * ROWS])
        for i in range(count)
    ]
    filt_real, filt_imag = spectra[-1]
    real_parts, imag_parts = [], []
    sum_real, sum_imag = None, None
    for one in range(sequences):
        mixed_real, mixed_imag = spectra[2 * one]
        gated_real, gated_imag = spectra[2 * one + 1]
        real_parts.append(mixed_real * filt_real - mixed_imag * filt_imag)
        imag_parts.append(mixed_real * filt_imag + mixed_imag * filt_real)
        real_parts.append(gated_real * filt_real + gated_imag * filt_imag)
        imag_parts.append(gated_imag * filt_real - gated_real * filt_imag)
        part_real = gated_real * mixed_real + gated_imag * mixed_imag
        part_imag = gated_imag * mixed_real - gated_real * mixed_imag
        sum_real = part_real if one == 0 else sum_real + part_real
        sum_imag = part_imag if one == 0 else sum_imag + part_imag
    real_parts.append(sum_real)
    imag_parts.append(sum_imag)
    high, low = halves(jnp.concatenate(real_parts + imag_parts, axis=0))
    by_cos = times_table(high, low, table_ref, 0)
    by_sin = times_table(high, low, table_ref, 2)
    back_real = by_cos[:half] - by_sin[half:]
    back_imag = by_cos[half:] + by_sin[:half]
    results = []
    for i in range(count):
        real = back_real[i * ROWS : (i + 1) * ROWS]
        imag = back_imag[i * ROWS : (i + 1) * ROWS]
        turned = jnp.concatenate(
            [real * turn_cos - imag * turn_sin, imag * turn_cos + real * turn_sin], axis=0
        )
        high, low = halves(turned)
        value = dot(leave_ref[0], high) + dot(leave_ref[0], low) + dot(leave_ref[1], high)
        results.append(value.astype(jnp.bfloat16))
    for one in range(sequences):
        rows = slice(one * BLOCKS, (one + 1) * BLOCKS)
        out_ref[rows, :WIDTH] = results[2 * one]
        out_ref[rows, WIDTH : 2 * WIDTH] = results[2 * one + 1]
        out_ref[rows, 2 * WIDTH :] = results[-1]


def convolve(rows_in):
    return pl.pallas_call(
        convolve_kernel,
        out_shape=jax.ShapeDtypeStruct(rows_in.shape, jnp.bfloat16),
        in_specs=[pl.BlockSpec(memory_space=pltpu.VMEM)] * 6,
        out_specs=pl.BlockSpec(memory_space=pltpu.VMEM),
        compiler_params=pltpu.CompilerParams(vmem_limit_bytes=32 * 1024 * 1024),
        name="convolve",
    )(rows_in, *(jnp.asarray(t) for t in tables()))


def exchange(rows):
    count, width = rows.shape
    moved = lax.all_to_all(
        rows.reshape(count, 2, width // 2), GROUP, split_axis=0, concat_axis=0, tiled=True
    )
    return moved.reshape(count, width)


def body(query_gate, key_gate, values_in, grad_out, long_filter):
    key_wide = key_gate[0].astype(jnp.float32)
    values_wide = values_in[0].astype(jnp.float32)
    grad_wide = grad_out[0].astype(jnp.float32)
    mixed_in = (key_wide * values_wide).astype(jnp.bfloat16)
    gated_grad = (grad_wide * query_gate[0].astype(jnp.float32)).astype(jnp.bfloat16)
    packed = jnp.concatenate([mixed_in.T, gated_grad.T, long_filter.T], axis=1)
    moved = exchange(packed)
    result = convolve(moved)
    returned = exchange(result)
    part = returned[:, 2 * WIDTH :]
    other = lax.ppermute(part, CORE, [(0, 1), (1, 0)])
    conv_out = returned[:, :WIDTH].T.astype(jnp.float32)
    grad_mixed = returned[:, WIDTH : 2 * WIDTH].T.astype(jnp.float32)
    grad_query = (grad_wide * conv_out).astype(jnp.bfloat16)
    grad_key = (grad_mixed * values_wide).astype(jnp.bfloat16)
    grad_value = (grad_mixed * key_wide).astype(jnp.bfloat16)
    grad_filter = (part.astype(jnp.float32) + other.astype(jnp.float32)).T
    return (grad_query[None], grad_key[None], grad_value[None], grad_filter)


def solution(mesh):
    fine = Mesh(mesh.devices.reshape(SIZES), (HI, CORE, LO, Y, X))
    whole = P((HI, CORE), SEQ_AXES, None)
    return jax.shard_map(
        body,
        mesh=fine,
        in_specs=(whole, whole, whole, whole, P(SEQ_AXES, None)),
        out_specs=(whole, whole, whole, P(SEQ_AXES, None)),
        check_vma=False,
    )
```

```python
import math

import jax
import jax.numpy as jnp
import numpy as np
from jax import lax
from jax.experimental import pallas as pl
from jax.experimental.pallas import tpu as pltpu
from jax.sharding import Mesh, PartitionSpec as P

HI, CORE, LO, Y, X = "hi", "core", "lo", "y", "x"
SIZES = (4, 2, 2, 8, 4)
SEQ_AXES = (LO, Y, X)
GROUP = (HI, LO, Y, X)
BLOCKS = 64
WIDTH = 256
ROWS = 64
LENGTH = 2 * BLOCKS * WIDTH


def split_bf16(array):
    high = array.astype(jnp.bfloat16)
    low = (array - high.astype(np.float32)).astype(jnp.bfloat16)
    return high, low


def tables():
    freq = np.arange(ROWS)[:, None] + 0.5
    block = np.arange(BLOCKS)[None, :]
    place = np.arange(WIDTH)
    angle = 2.0 * math.pi * freq * block / (2 * BLOCKS)
    enter = np.concatenate([np.cos(angle), -np.sin(angle)], axis=0).astype(np.float32)
    scale = 2.0 / LENGTH / math.sqrt(BLOCKS * WIDTH)
    leave = (scale * np.concatenate([np.cos(angle.T), -np.sin(angle.T)], axis=1)).astype(np.float32)
    turn = 2.0 * math.pi * freq * place[None, :] / LENGTH
    angle = 2.0 * math.pi * (place[:, None] * place[None, :] % WIDTH) / WIDTH
    cos_high, cos_low = split_bf16(np.cos(angle).astype(np.float32))
    sin_high, sin_low = split_bf16(np.sin(angle).astype(np.float32))
    leave_high, leave_low = split_bf16(leave)
    return (
        np.concatenate(split_bf16(enter), axis=1),
        np.cos(turn).astype(np.float32),
        np.sin(turn).astype(np.float32),
        np.stack([cos_high, cos_low, sin_high, sin_low]),
        np.concatenate([leave_high, leave_high, leave_low], axis=1),
    )


def dot(left, right):
    return jnp.dot(left, right, preferred_element_type=jnp.float32)


def halves(array):
    high = array.astype(jnp.bfloat16)
    return high, (array - high.astype(jnp.float32)).astype(jnp.bfloat16)


def turn_by(parts, high_table, low_table):
    high, low = halves(parts)
    return dot(
        jnp.concatenate([high, low, high], axis=1),
        jnp.concatenate([high_table, high_table, low_table], axis=0),
    )


def complex_table(cosine, sine):
    return jnp.concatenate(
        [jnp.concatenate([cosine, sine], axis=1), jnp.concatenate([-sine, cosine], axis=1)], axis=0
    )


def convolve_kernel(x_ref, enter_ref, cos_ref, sin_ref, table_ref, leave_ref, out_ref):
    sequences = x_ref.shape[0] // BLOCKS
    turn_cos, turn_sin = cos_ref[...], sin_ref[...]
    signals = []
    for one in range(sequences):
        rows = slice(one * BLOCKS, (one + 1) * BLOCKS)
        signals += [x_ref[rows, :WIDTH], x_ref[rows, WIDTH : 2 * WIDTH]]
    signals.append(x_ref[:BLOCKS, 2 * WIDTH :])
    count = len(signals)
    signals = jnp.concatenate(signals, axis=1)
    first = dot(enter_ref[...], jnp.concatenate([signals, signals], axis=0))
    parts = []
    for i in range(count):
        real = first[:ROWS, i * WIDTH : (i + 1) * WIDTH]
        imag = first[ROWS:, i * WIDTH : (i + 1) * WIDTH]
        parts.append(
            jnp.concatenate(
                [real * turn_cos + imag * turn_sin, imag * turn_cos - real * turn_sin], axis=1
            )
        )
    spectra = turn_by(
        jnp.concatenate(parts, axis=0),
        complex_table(table_ref[0], -table_ref[2]),
        complex_table(table_ref[1], -table_ref[3]),
    )

    def spectrum(i):
        rows = slice(i * ROWS, (i + 1) * ROWS)
        return spectra[rows, :WIDTH], spectra[rows, WIDTH:]

    filt_real, filt_imag = spectrum(count - 1)
    parts = []
    total = None
    for one in range(sequences):
        mixed_real, mixed_imag = spectrum(2 * one)
        gated_real, gated_imag = spectrum(2 * one + 1)
        parts.append(
            jnp.concatenate(
                [
                    mixed_real * filt_real - mixed_imag * filt_imag,
                    mixed_real * filt_imag + mixed_imag * filt_real,
                ],
                axis=1,
            )
        )
        parts.append(
            jnp.concatenate(
                [
                    gated_real * filt_real + gated_imag * filt_imag,
                    gated_imag * filt_real - gated_real * filt_imag,
                ],
                axis=1,
            )
        )
        part = jnp.concatenate(
            [
                gated_real * mixed_real + gated_imag * mixed_imag,
                gated_imag * mixed_real - gated_real * mixed_imag,
            ],
            axis=1,
        )
        total = part if one == 0 else total + part
    parts.append(total)
    back = turn_by(
        jnp.concatenate(parts, axis=0),
        complex_table(table_ref[0], table_ref[2]),
        complex_table(table_ref[1], table_ref[3]),
    )
    turned = []
    for i in range(count):
        real = back[i * ROWS : (i + 1) * ROWS, :WIDTH]
        imag = back[i * ROWS : (i + 1) * ROWS, WIDTH:]
        turned.append(
            jnp.concatenate(
                [real * turn_cos - imag * turn_sin, imag * turn_cos + real * turn_sin], axis=0
            )
        )
    high, low = halves(jnp.concatenate(turned, axis=1))
    values = dot(leave_ref[...], jnp.concatenate([high, low, high], axis=0)).astype(jnp.bfloat16)
    for one in range(sequences):
        rows = slice(one * BLOCKS, (one + 1) * BLOCKS)
        out_ref[rows, : 2 * WIDTH] = values[:, 2 * one * WIDTH : 2 * (one + 1) * WIDTH]
        out_ref[rows, 2 * WIDTH :] = values[:, (count - 1) * WIDTH :]


def convolve(rows_in):
    return pl.pallas_call(
        convolve_kernel,
        out_shape=jax.ShapeDtypeStruct(rows_in.shape, jnp.bfloat16),
        in_specs=[pl.BlockSpec(memory_space=pltpu.VMEM)] * 6,
        out_specs=pl.BlockSpec(memory_space=pltpu.VMEM),
        compiler_params=pltpu.CompilerParams(vmem_limit_bytes=32 * 1024 * 1024),
        name="convolve",
    )(rows_in, *(jnp.asarray(t) for t in tables()))


def exchange(rows):
    count, width = rows.shape
    moved = lax.all_to_all(
        rows.reshape(count, 2, width // 2), GROUP, split_axis=0, concat_axis=0, tiled=True
    )
    return moved.reshape(count, width)


def body(query_gate, key_gate, values_in, grad_out, long_filter):
    key_wide = key_gate[0].astype(jnp.float32)
    values_wide = values_in[0].astype(jnp.float32)
    grad_wide = grad_out[0].astype(jnp.float32)
    mixed_in = (key_wide * values_wide).astype(jnp.bfloat16)
    gated_grad = (grad_wide * query_gate[0].astype(jnp.float32)).astype(jnp.bfloat16)
    packed = jnp.concatenate([mixed_in.T, gated_grad.T, long_filter.T], axis=1)
    moved = exchange(packed)
    result = convolve(moved)
    returned = exchange(result)
    part = returned[:, 2 * WIDTH :]
    other = lax.ppermute(part, CORE, [(0, 1), (1, 0)])
    conv_out = returned[:, :WIDTH].T.astype(jnp.float32)
    grad_mixed = returned[:, WIDTH : 2 * WIDTH].T.astype(jnp.float32)
    grad_query = (grad_wide * conv_out).astype(jnp.bfloat16)
    grad_key = (grad_mixed * values_wide).astype(jnp.bfloat16)
    grad_value = (grad_mixed * key_wide).astype(jnp.bfloat16)
    grad_filter = (part.astype(jnp.float32) + other.astype(jnp.float32)).T
    return (grad_query[None], grad_key[None], grad_value[None], grad_filter)


def solution(mesh):
    fine = Mesh(mesh.devices.reshape(SIZES), (HI, CORE, LO, Y, X))
    whole = P((HI, CORE), SEQ_AXES, None)
    return jax.shard_map(
        body,
        mesh=fine,
        in_specs=(whole, whole, whole, whole, P(SEQ_AXES, None)),
        out_specs=(whole, whole, whole, P(SEQ_AXES, None)),
        check_vma=False,
    )
```

```python
import math

import jax
import jax.numpy as jnp
import numpy as np
from jax import lax
from jax.experimental import pallas as pl
from jax.experimental.pallas import tpu as pltpu
from jax.sharding import Mesh, PartitionSpec as P

HI, CORE, LO, Y, X = "hi", "core", "lo", "y", "x"
SIZES = (4, 2, 2, 8, 4)
SEQ_AXES = (LO, Y, X)
GROUP = (HI, LO, Y, X)
BLOCKS = 64
WIDTH = 256
ROWS = 64
LENGTH = 2 * BLOCKS * WIDTH


def split_bf16(array):
    high = array.astype(jnp.bfloat16)
    low = (array - high.astype(np.float32)).astype(jnp.bfloat16)
    return high, low


def tables():
    freq = np.arange(ROWS)[:, None] + 0.5
    block = np.arange(BLOCKS)[None, :]
    place = np.arange(WIDTH)
    angle = 2.0 * math.pi * freq * block / (2 * BLOCKS)
    enter = np.concatenate([np.cos(angle), -np.sin(angle)], axis=0).astype(np.float32)
    scale = 2.0 / LENGTH / math.sqrt(BLOCKS * WIDTH)
    leave = (scale * np.concatenate([np.cos(angle.T), -np.sin(angle.T)], axis=1)).astype(np.float32)
    turn = 2.0 * math.pi * freq * place[None, :] / LENGTH
    angle = 2.0 * math.pi * (place[:, None] * place[None, :] % WIDTH) / WIDTH
    cos_high, cos_low = split_bf16(np.cos(angle).astype(np.float32))
    sin_high, sin_low = split_bf16(np.sin(angle).astype(np.float32))
    enter = np.concatenate(split_bf16(enter), axis=1)
    coarse = np.concatenate(
        [
            cos_high[: WIDTH // 2],
            cos_low[: WIDTH // 2],
            sin_high[: WIDTH // 2],
            sin_low[: WIDTH // 2],
            np.pad(enter, ((0, 0), (0, WIDTH - enter.shape[1]))),
            np.concatenate(split_bf16(leave), axis=1),
        ],
        axis=0,
    )
    fine = np.concatenate([np.cos(turn), np.sin(turn)], axis=0).astype(np.float32)
    return coarse, fine


def dot(left, right):
    return jnp.dot(left, right, preferred_element_type=jnp.float32)


def halves(array):
    high = array.astype(jnp.bfloat16)
    return high, (array - high.astype(jnp.float32)).astype(jnp.bfloat16)


def turn_by(parts, high_table, low_table):
    high, low = halves(parts)
    return dot(
        jnp.concatenate([high, low, high], axis=1),
        jnp.concatenate([high_table, high_table, low_table], axis=0),
    )


def complex_table(cosine, sine):
    return jnp.concatenate(
        [jnp.concatenate([cosine, sine], axis=1), jnp.concatenate([-sine, cosine], axis=1)], axis=0
    )


def convolve_kernel(x_ref, coarse_ref, fine_ref, out_ref):
    cos_high, cos_low, sin_high, sin_low = (
        coarse_ref[i * WIDTH : (i + 1) * WIDTH] for i in range(4)
    )
    at = 4 * WIDTH
    enter = coarse_ref[at : at + 2 * ROWS, : 2 * BLOCKS]
    leave_high = coarse_ref[at + 2 * ROWS : at + 2 * ROWS + BLOCKS, : 2 * ROWS]
    leave_low = coarse_ref[at + 2 * ROWS : at + 2 * ROWS + BLOCKS, 2 * ROWS :]
    leave = jnp.concatenate([leave_high, leave_high, leave_low], axis=1)
    sequences = x_ref.shape[0] // BLOCKS
    turn_cos, turn_sin = fine_ref[:ROWS], fine_ref[ROWS:]
    signals = []
    for one in range(sequences):
        rows = slice(one * BLOCKS, (one + 1) * BLOCKS)
        signals += [x_ref[rows, :WIDTH], x_ref[rows, WIDTH : 2 * WIDTH]]
    signals.append(x_ref[:BLOCKS, 2 * WIDTH :])
    count = len(signals)
    signals = jnp.concatenate(signals, axis=1)
    first = dot(enter, jnp.concatenate([signals, signals], axis=0))
    parts = []
    for i in range(count):
        real = first[:ROWS, i * WIDTH : (i + 1) * WIDTH]
        imag = first[ROWS:, i * WIDTH : (i + 1) * WIDTH]
        parts.append(
            jnp.concatenate(
                [real * turn_cos + imag * turn_sin, imag * turn_cos - real * turn_sin], axis=1
            )
        )
    spectra = turn_by(
        jnp.concatenate(parts, axis=0),
        complex_table(cos_high, -sin_high),
        complex_table(cos_low, -sin_low),
    )

    def spectrum(i):
        rows = slice(i * ROWS, (i + 1) * ROWS)
        return spectra[rows, :WIDTH], spectra[rows, WIDTH:]

    filt_real, filt_imag = spectrum(count - 1)
    parts = []
    total = None
    for one in range(sequences):
        mixed_real, mixed_imag = spectrum(2 * one)
        gated_real, gated_imag = spectrum(2 * one + 1)
        parts.append(
            jnp.concatenate(
                [
                    mixed_real * filt_real - mixed_imag * filt_imag,
                    mixed_real * filt_imag + mixed_imag * filt_real,
                ],
                axis=1,
            )
        )
        parts.append(
            jnp.concatenate(
                [
                    gated_real * filt_real + gated_imag * filt_imag,
                    gated_imag * filt_real - gated_real * filt_imag,
                ],
                axis=1,
            )
        )
        part = jnp.concatenate(
            [
                gated_real * mixed_real + gated_imag * mixed_imag,
                gated_imag * mixed_real - gated_real * mixed_imag,
            ],
            axis=1,
        )
        total = part if one == 0 else total + part
    parts.append(total)
    back = turn_by(
        jnp.concatenate(parts, axis=0),
        complex_table(cos_high, sin_high),
        complex_table(cos_low, sin_low),
    )
    turned = []
    for i in range(count):
        real = back[i * ROWS : (i + 1) * ROWS, :WIDTH]
        imag = back[i * ROWS : (i + 1) * ROWS, WIDTH:]
        turned.append(
            jnp.concatenate(
                [real * turn_cos - imag * turn_sin, imag * turn_cos + real * turn_sin], axis=0
            )
        )
    high, low = halves(jnp.concatenate(turned, axis=1))
    values = dot(leave, jnp.concatenate([high, low, high], axis=0)).astype(jnp.bfloat16)
    for one in range(sequences):
        rows = slice(one * BLOCKS, (one + 1) * BLOCKS)
        out_ref[rows, : 2 * WIDTH] = values[:, 2 * one * WIDTH : 2 * (one + 1) * WIDTH]
        out_ref[rows, 2 * WIDTH :] = values[:, (count - 1) * WIDTH :]


def convolve(rows_in, held):
    return pl.pallas_call(
        convolve_kernel,
        out_shape=jax.ShapeDtypeStruct(rows_in.shape, jnp.bfloat16),
        in_specs=[pl.BlockSpec(memory_space=pltpu.VMEM)] * 3,
        out_specs=pl.BlockSpec(memory_space=pltpu.VMEM),
        compiler_params=pltpu.CompilerParams(vmem_limit_bytes=32 * 1024 * 1024),
        name="convolve",
    )(rows_in, *held)


def flip(array):
    size = array.shape[1]
    row = lax.broadcasted_iota(jnp.int32, (size, size), 0)
    column = lax.broadcasted_iota(jnp.int32, (size, size), 1)
    identity = jnp.where(row == column, 1.0, 0.0).astype(jnp.bfloat16)
    return lax.dot_general(
        identity, array, (((1,), (1,)), ((), ())), preferred_element_type=jnp.float32
    )


def pack_kernel(mixed_ref, gated_ref, filter_ref, coarse_ref, fine_ref, packed_ref, *held_refs):
    held_coarse_ref, held_fine_ref = held_refs
    for at, part_ref in enumerate((mixed_ref, gated_ref, filter_ref)):
        packed_ref[:, at * WIDTH : (at + 1) * WIDTH] = flip(part_ref[...]).astype(jnp.bfloat16)
    half = WIDTH // 2
    odd = lax.broadcasted_iota(jnp.int32, (half, WIDTH), 1) % 2 == 1
    for i in range(4):
        rows = coarse_ref[i * half : (i + 1) * half].astype(jnp.float32)
        both = jnp.concatenate([rows, jnp.where(odd, -rows, rows)], axis=0)
        held_coarse_ref[i * WIDTH : (i + 1) * WIDTH] = both.astype(jnp.bfloat16)
    held_coarse_ref[4 * WIDTH :] = coarse_ref[4 * half :]
    held_fine_ref[...] = fine_ref[...]


def pack(mixed_in, gated_grad, long_filter):
    coarse, fine = (jnp.asarray(t) for t in tables())
    packed, *held = pl.pallas_call(
        pack_kernel,
        out_shape=[
            jax.ShapeDtypeStruct((WIDTH, 3 * WIDTH), jnp.bfloat16),
            jax.ShapeDtypeStruct((coarse.shape[0] + 2 * WIDTH, WIDTH), jnp.bfloat16),
            jax.ShapeDtypeStruct(fine.shape, jnp.float32),
        ],
        in_specs=[pl.BlockSpec(memory_space=pltpu.VMEM)] * 5,
        out_specs=[pl.BlockSpec(memory_space=pltpu.VMEM)] * 3,
        compiler_params=pltpu.CompilerParams(vmem_limit_bytes=32 * 1024 * 1024),
        name="pack",
    )(mixed_in, gated_grad, long_filter, coarse, fine)
    return packed, held


def exchange(rows):
    count, width = rows.shape
    moved = lax.all_to_all(
        rows.reshape(count, 2, width // 2), GROUP, split_axis=0, concat_axis=0, tiled=True
    )
    return moved.reshape(count, width)


def body(query_gate, key_gate, values_in, grad_out, long_filter):
    key_wide = key_gate[0].astype(jnp.float32)
    values_wide = values_in[0].astype(jnp.float32)
    grad_wide = grad_out[0].astype(jnp.float32)
    mixed_in = (key_wide * values_wide).astype(jnp.bfloat16)
    gated_grad = (grad_wide * query_gate[0].astype(jnp.float32)).astype(jnp.bfloat16)
    packed, held = pack(mixed_in, gated_grad, long_filter)
    moved = exchange(packed)
    result = convolve(moved, held)
    returned = exchange(result)
    part = returned[:, 2 * WIDTH :]
    other = lax.ppermute(part, CORE, [(0, 1), (1, 0)])
    conv_out = returned[:, :WIDTH].T.astype(jnp.float32)
    grad_mixed = returned[:, WIDTH : 2 * WIDTH].T.astype(jnp.float32)
    grad_query = (grad_wide * conv_out).astype(jnp.bfloat16)
    grad_key = (grad_mixed * values_wide).astype(jnp.bfloat16)
    grad_value = (grad_mixed * key_wide).astype(jnp.bfloat16)
    grad_filter = (part.astype(jnp.float32) + other.astype(jnp.float32)).T
    return (grad_query[None], grad_key[None], grad_value[None], grad_filter)


def solution(mesh):
    fine = Mesh(mesh.devices.reshape(SIZES), (HI, CORE, LO, Y, X))
    whole = P((HI, CORE), SEQ_AXES, None)
    return jax.shard_map(
        body,
        mesh=fine,
        in_specs=(whole, whole, whole, whole, P(SEQ_AXES, None)),
        out_specs=(whole, whole, whole, P(SEQ_AXES, None)),
        check_vma=False,
    )
```

```python
import math

import jax
import jax.numpy as jnp
import numpy as np
from jax import lax
from jax.experimental import pallas as pl
from jax.experimental.pallas import tpu as pltpu
from jax.sharding import Mesh, PartitionSpec as P

HI, CORE, LO, Y, X = "hi", "core", "lo", "y", "x"
SIZES = (4, 2, 2, 8, 4)
SEQ_AXES = (LO, Y, X)
GROUP = (HI, LO, Y, X)
BLOCKS = 64
WIDTH = 256
ROWS = 64
LENGTH = 2 * BLOCKS * WIDTH


def split_bf16(array):
    high = array.astype(jnp.bfloat16)
    low = (array - high.astype(np.float32)).astype(jnp.bfloat16)
    return high, low


def tables():
    freq = np.arange(ROWS)[:, None] + 0.5
    block = np.arange(BLOCKS)[None, :]
    place = np.arange(WIDTH)
    angle = 2.0 * math.pi * freq * block / (2 * BLOCKS)
    enter = np.concatenate([np.cos(angle), -np.sin(angle)], axis=0).astype(np.float32)
    scale = 2.0 / LENGTH / math.sqrt(BLOCKS * WIDTH)
    leave = (scale * np.concatenate([np.cos(angle.T), -np.sin(angle.T)], axis=1)).astype(np.float32)
    turn = 2.0 * math.pi * freq * place[None, :] / LENGTH
    angle = 2.0 * math.pi * (place[:, None] * place[None, :] % WIDTH) / WIDTH
    cos_high, cos_low = split_bf16(np.cos(angle).astype(np.float32))
    sin_high, sin_low = split_bf16(np.sin(angle).astype(np.float32))
    enter = np.concatenate(split_bf16(enter), axis=1)
    coarse = np.concatenate(
        [
            cos_high[: WIDTH // 2],
            cos_low[: WIDTH // 2],
            sin_high[: WIDTH // 2],
            sin_low[: WIDTH // 2],
            np.pad(enter, ((0, 0), (0, WIDTH - enter.shape[1]))),
            np.concatenate(split_bf16(leave), axis=1),
        ],
        axis=0,
    )
    fine = np.concatenate([np.cos(turn), np.sin(turn)], axis=0).astype(np.float32)
    return coarse, fine


def dot(left, right):
    return jnp.dot(left, right, preferred_element_type=jnp.float32)


def halves(array):
    high = array.astype(jnp.bfloat16)
    return high, (array - high.astype(jnp.float32)).astype(jnp.bfloat16)


def turn_by(parts, high_table, low_table):
    high, low = halves(parts)
    return dot(
        jnp.concatenate([high, low, high], axis=1),
        jnp.concatenate([high_table, high_table, low_table], axis=0),
    )


def complex_table(cosine, sine):
    return jnp.concatenate(
        [jnp.concatenate([cosine, sine], axis=1), jnp.concatenate([-sine, cosine], axis=1)], axis=0
    )


def convolve_kernel(x_ref, coarse_ref, fine_ref, out_ref, part_ref):
    cos_high, cos_low, sin_high, sin_low = (
        coarse_ref[i * WIDTH : (i + 1) * WIDTH] for i in range(4)
    )
    at = 4 * WIDTH
    enter = coarse_ref[at : at + 2 * ROWS, : 2 * BLOCKS]
    leave_high = coarse_ref[at + 2 * ROWS : at + 2 * ROWS + BLOCKS, : 2 * ROWS]
    leave_low = coarse_ref[at + 2 * ROWS : at + 2 * ROWS + BLOCKS, 2 * ROWS :]
    leave = jnp.concatenate([leave_high, leave_high, leave_low], axis=1)
    sequences = x_ref.shape[0] // BLOCKS
    turn_cos, turn_sin = fine_ref[:ROWS], fine_ref[ROWS:]
    signals = []
    for one in range(sequences):
        rows = slice(one * BLOCKS, (one + 1) * BLOCKS)
        signals += [x_ref[rows, :WIDTH], x_ref[rows, WIDTH : 2 * WIDTH]]
    signals.append(x_ref[:BLOCKS, 2 * WIDTH :])
    count = len(signals)
    signals = jnp.concatenate(signals, axis=1)
    first = dot(enter, jnp.concatenate([signals, signals], axis=0))
    parts = []
    for i in range(count):
        real = first[:ROWS, i * WIDTH : (i + 1) * WIDTH]
        imag = first[ROWS:, i * WIDTH : (i + 1) * WIDTH]
        parts.append(
            jnp.concatenate(
                [real * turn_cos + imag * turn_sin, imag * turn_cos - real * turn_sin], axis=1
            )
        )
    spectra = turn_by(
        jnp.concatenate(parts, axis=0),
        complex_table(cos_high, -sin_high),
        complex_table(cos_low, -sin_low),
    )

    def spectrum(i):
        rows = slice(i * ROWS, (i + 1) * ROWS)
        return spectra[rows, :WIDTH], spectra[rows, WIDTH:]

    filt_real, filt_imag = spectrum(count - 1)
    parts = []
    total = None
    for one in range(sequences):
        mixed_real, mixed_imag = spectrum(2 * one)
        gated_real, gated_imag = spectrum(2 * one + 1)
        parts.append(
            jnp.concatenate(
                [
                    mixed_real * filt_real - mixed_imag * filt_imag,
                    mixed_real * filt_imag + mixed_imag * filt_real,
                ],
                axis=1,
            )
        )
        parts.append(
            jnp.concatenate(
                [
                    gated_real * filt_real + gated_imag * filt_imag,
                    gated_imag * filt_real - gated_real * filt_imag,
                ],
                axis=1,
            )
        )
        part = jnp.concatenate(
            [
                gated_real * mixed_real + gated_imag * mixed_imag,
                gated_imag * mixed_real - gated_real * mixed_imag,
            ],
            axis=1,
        )
        total = part if one == 0 else total + part
    parts.append(total)
    back = turn_by(
        jnp.concatenate(parts, axis=0),
        complex_table(cos_high, sin_high),
        complex_table(cos_low, sin_low),
    )
    turned = []
    for i in range(count):
        real = back[i * ROWS : (i + 1) * ROWS, :WIDTH]
        imag = back[i * ROWS : (i + 1) * ROWS, WIDTH:]
        turned.append(
            jnp.concatenate(
                [real * turn_cos - imag * turn_sin, imag * turn_cos + real * turn_sin], axis=0
            )
        )
    high, low = halves(jnp.concatenate(turned, axis=1))
    values = dot(leave, jnp.concatenate([high, low, high], axis=0))
    for one in range(sequences):
        rows = slice(one * BLOCKS, (one + 1) * BLOCKS)
        columns = slice(2 * one * WIDTH, 2 * (one + 1) * WIDTH)
        out_ref[rows] = values[:, columns].astype(jnp.bfloat16)
    part_ref[...] = values[:, (count - 1) * WIDTH :]


def local_call(kernel, name, outputs, *operands):
    return pl.pallas_call(
        kernel,
        out_shape=[jax.ShapeDtypeStruct(shape, dtype) for shape, dtype in outputs],
        in_specs=[pl.BlockSpec(memory_space=pltpu.VMEM)] * len(operands),
        out_specs=[pl.BlockSpec(memory_space=pltpu.VMEM)] * len(outputs),
        compiler_params=pltpu.CompilerParams(vmem_limit_bytes=32 * 1024 * 1024),
        name=name,
    )(*operands)


def convolve(rows_in, held):
    outputs = [((rows_in.shape[0], 2 * WIDTH), jnp.bfloat16), ((BLOCKS, WIDTH), jnp.float32)]
    return local_call(convolve_kernel, "convolve", outputs, rows_in, *held)


def merge_kernel(rows_ref, part_ref, other_ref, *refs):
    count = len(refs) // 2
    out_ref = refs[count]
    total = (part_ref[...] + other_ref[...]).astype(jnp.bfloat16)
    out_ref[:, : 2 * WIDTH] = rows_ref[...]
    for at in range(0, rows_ref.shape[0], BLOCKS):
        out_ref[at : at + BLOCKS, 2 * WIDTH :] = total
    for source, target in zip(refs[:count], refs[count + 1 :]):
        target[...] = source[...]


def merge(rows, part, other, *arrays):
    outputs = [((rows.shape[0], 3 * WIDTH), jnp.bfloat16)]
    outputs += [(array.shape, array.dtype) for array in arrays]
    return local_call(merge_kernel, "merge", outputs, rows, part, other, *arrays)


def finish_kernel(
    rows_ref, key_ref, values_ref, grad_ref, query_out, key_out, value_out, filter_out
):
    conv_out = flip(rows_ref[:, :WIDTH])
    query_out[0] = (grad_ref[0].astype(jnp.float32) * conv_out).astype(jnp.bfloat16)
    grad_mixed = flip(rows_ref[:, WIDTH : 2 * WIDTH])
    key_out[0] = (grad_mixed * values_ref[0].astype(jnp.float32)).astype(jnp.bfloat16)
    value_out[0] = (grad_mixed * key_ref[0].astype(jnp.float32)).astype(jnp.bfloat16)
    filter_out[...] = flip(rows_ref[:, 2 * WIDTH :])


def finish(rows, *arrays):
    outputs = [(array.shape, jnp.bfloat16) for array in arrays] + [((WIDTH, WIDTH), jnp.float32)]
    return local_call(finish_kernel, "finish", outputs, rows, *arrays)


def flip(array):
    size = array.shape[1]
    row = lax.broadcasted_iota(jnp.int32, (size, size), 0)
    column = lax.broadcasted_iota(jnp.int32, (size, size), 1)
    identity = jnp.where(row == column, 1.0, 0.0).astype(jnp.bfloat16)
    return lax.dot_general(
        identity, array, (((1,), (1,)), ((), ())), preferred_element_type=jnp.float32
    )


def pack_kernel(mixed_ref, gated_ref, filter_ref, coarse_ref, fine_ref, packed_ref, *held_refs):
    held_coarse_ref, held_fine_ref = held_refs
    for at, part_ref in enumerate((mixed_ref, gated_ref, filter_ref)):
        packed_ref[:, at * WIDTH : (at + 1) * WIDTH] = flip(part_ref[...]).astype(jnp.bfloat16)
    half = WIDTH // 2
    odd = lax.broadcasted_iota(jnp.int32, (half, WIDTH), 1) % 2 == 1
    for i in range(4):
        rows = coarse_ref[i * half : (i + 1) * half].astype(jnp.float32)
        both = jnp.concatenate([rows, jnp.where(odd, -rows, rows)], axis=0)
        held_coarse_ref[i * WIDTH : (i + 1) * WIDTH] = both.astype(jnp.bfloat16)
    held_coarse_ref[4 * WIDTH :] = coarse_ref[4 * half :]
    held_fine_ref[...] = fine_ref[...]


def pack(mixed_in, gated_grad, long_filter):
    coarse, fine = (jnp.asarray(t) for t in tables())
    packed, *held = pl.pallas_call(
        pack_kernel,
        out_shape=[
            jax.ShapeDtypeStruct((WIDTH, 3 * WIDTH), jnp.bfloat16),
            jax.ShapeDtypeStruct((coarse.shape[0] + 2 * WIDTH, WIDTH), jnp.bfloat16),
            jax.ShapeDtypeStruct(fine.shape, jnp.float32),
        ],
        in_specs=[pl.BlockSpec(memory_space=pltpu.VMEM)] * 5,
        out_specs=[pl.BlockSpec(memory_space=pltpu.VMEM)] * 3,
        compiler_params=pltpu.CompilerParams(vmem_limit_bytes=32 * 1024 * 1024),
        name="pack",
    )(mixed_in, gated_grad, long_filter, coarse, fine)
    return packed, held


def exchange(rows):
    count, width = rows.shape
    moved = lax.all_to_all(
        rows.reshape(count, 2, width // 2), GROUP, split_axis=0, concat_axis=0, tiled=True
    )
    return moved.reshape(count, width)


def body(query_gate, key_gate, values_in, grad_out, long_filter):
    mixed_in = (key_gate[0].astype(jnp.float32) * values_in[0].astype(jnp.float32)).astype(
        jnp.bfloat16
    )
    gated_grad = (grad_out[0].astype(jnp.float32) * query_gate[0].astype(jnp.float32)).astype(
        jnp.bfloat16
    )
    packed, held = pack(mixed_in, gated_grad, long_filter)
    result, part = convolve(exchange(packed), held)
    other = lax.ppermute(part, CORE, [(0, 1), (1, 0)])
    merged, *arrays = merge(result, part, other, key_gate, values_in, grad_out)
    return tuple(finish(exchange(merged), *arrays))


def solution(mesh):
    fine = Mesh(mesh.devices.reshape(SIZES), (HI, CORE, LO, Y, X))
    whole = P((HI, CORE), SEQ_AXES, None)
    return jax.shard_map(
        body,
        mesh=fine,
        in_specs=(whole, whole, whole, whole, P(SEQ_AXES, None)),
        out_specs=(whole, whole, whole, P(SEQ_AXES, None)),
        check_vma=False,
    )
```

```python
import math

import jax
import jax.numpy as jnp
import numpy as np
from jax import lax
from jax.experimental import pallas as pl
from jax.experimental.pallas import tpu as pltpu
from jax.sharding import Mesh, PartitionSpec as P

HI, CORE, LO, Y, X = "hi", "core", "lo", "y", "x"
SIZES = (4, 2, 2, 8, 4)
SEQ_AXES = (LO, Y, X)
AXES = (HI, CORE, LO, Y, X)
BLOCKS = 64
WIDTH = 256
ROWS = 64
LENGTH = 2 * BLOCKS * WIDTH


def split_bf16(array):
    high = array.astype(jnp.bfloat16)
    low = (array - high.astype(np.float32)).astype(jnp.bfloat16)
    return high, low


def tables():
    freq = np.arange(ROWS)[:, None] + 0.5
    block = np.arange(BLOCKS)[None, :]
    place = np.arange(WIDTH)
    angle = 2.0 * math.pi * freq * block / (2 * BLOCKS)
    enter = np.concatenate([np.cos(angle), -np.sin(angle)], axis=0).astype(np.float32)
    scale = 2.0 / LENGTH / math.sqrt(BLOCKS * WIDTH)
    leave = (scale * np.concatenate([np.cos(angle.T), -np.sin(angle.T)], axis=1)).astype(np.float32)
    turn = 2.0 * math.pi * freq * place[None, :] / LENGTH
    angle = 2.0 * math.pi * (place[:, None] * place[None, :] % WIDTH) / WIDTH
    cos_high, cos_low = split_bf16(np.cos(angle).astype(np.float32))
    sin_high, sin_low = split_bf16(np.sin(angle).astype(np.float32))
    forward, backward = enter, enter[:, ::-1]
    coarse = np.concatenate(
        [
            cos_high[: WIDTH // 2],
            cos_low[: WIDTH // 2],
            sin_high[: WIDTH // 2],
            sin_low[: WIDTH // 2],
            np.concatenate(split_bf16(forward) + split_bf16(backward), axis=1),
            np.concatenate(split_bf16(leave), axis=1),
            np.concatenate(split_bf16(leave[::-1]), axis=1),
        ],
        axis=0,
    )
    fine = np.concatenate([np.cos(turn), np.sin(turn)], axis=0).astype(np.float32)
    return coarse, fine


def dot(left, right):
    return jnp.dot(left, right, preferred_element_type=jnp.float32)


def halves(array):
    high = array.astype(jnp.bfloat16)
    return high, (array - high.astype(jnp.float32)).astype(jnp.bfloat16)


def turn_by(parts, high_table, low_table):
    high, low = halves(parts)
    return dot(
        jnp.concatenate([high, low, high], axis=1),
        jnp.concatenate([high_table, high_table, low_table], axis=0),
    )


def complex_table(cosine, sine):
    return jnp.concatenate(
        [jnp.concatenate([cosine, sine], axis=1), jnp.concatenate([-sine, cosine], axis=1)], axis=0
    )


def convolve_kernel(x_ref, coarse_ref, fine_ref, out_ref, part_ref):
    cos_high, cos_low, sin_high, sin_low = (
        coarse_ref[i * WIDTH : (i + 1) * WIDTH] for i in range(4)
    )
    at = 4 * WIDTH
    backward = runs_backward()
    enter = jnp.where(
        backward,
        coarse_ref[at : at + 2 * ROWS, 2 * BLOCKS :],
        coarse_ref[at : at + 2 * ROWS, : 2 * BLOCKS],
    )
    at += 2 * ROWS
    natural = coarse_ref[at : at + BLOCKS]
    leave = jnp.where(backward, coarse_ref[at + BLOCKS : at + 2 * BLOCKS], natural)
    natural, leave = (
        jnp.concatenate([both[:, : 2 * ROWS], both[:, : 2 * ROWS], both[:, 2 * ROWS :]], axis=1)
        for both in (natural, leave)
    )
    sequences = x_ref.shape[0] // BLOCKS
    turn_cos, turn_sin = fine_ref[:ROWS], fine_ref[ROWS:]
    signals = []
    for one in range(sequences):
        rows = slice(one * BLOCKS, (one + 1) * BLOCKS)
        signals += [x_ref[rows, :WIDTH], x_ref[rows, WIDTH : 2 * WIDTH]]
    signals.append(x_ref[:BLOCKS, 2 * WIDTH :])
    count = len(signals)
    signals = jnp.concatenate(signals, axis=1)
    first = dot(enter, jnp.concatenate([signals, signals], axis=0))
    parts = []
    for i in range(count):
        real = first[:ROWS, i * WIDTH : (i + 1) * WIDTH]
        imag = first[ROWS:, i * WIDTH : (i + 1) * WIDTH]
        parts.append(
            jnp.concatenate(
                [real * turn_cos + imag * turn_sin, imag * turn_cos - real * turn_sin], axis=1
            )
        )
    spectra = turn_by(
        jnp.concatenate(parts, axis=0),
        complex_table(cos_high, -sin_high),
        complex_table(cos_low, -sin_low),
    )

    def spectrum(i):
        rows = slice(i * ROWS, (i + 1) * ROWS)
        return spectra[rows, :WIDTH], spectra[rows, WIDTH:]

    filt_real, filt_imag = spectrum(count - 1)
    parts = []
    total = None
    for one in range(sequences):
        mixed_real, mixed_imag = spectrum(2 * one)
        gated_real, gated_imag = spectrum(2 * one + 1)
        parts.append(
            jnp.concatenate(
                [
                    mixed_real * filt_real - mixed_imag * filt_imag,
                    mixed_real * filt_imag + mixed_imag * filt_real,
                ],
                axis=1,
            )
        )
        parts.append(
            jnp.concatenate(
                [
                    gated_real * filt_real + gated_imag * filt_imag,
                    gated_imag * filt_real - gated_real * filt_imag,
                ],
                axis=1,
            )
        )
        part = jnp.concatenate(
            [
                gated_real * mixed_real + gated_imag * mixed_imag,
                gated_imag * mixed_real - gated_real * mixed_imag,
            ],
            axis=1,
        )
        total = part if one == 0 else total + part
    parts.append(total)
    back = turn_by(
        jnp.concatenate(parts, axis=0),
        complex_table(cos_high, sin_high),
        complex_table(cos_low, sin_low),
    )
    turned = []
    for i in range(count):
        real = back[i * ROWS : (i + 1) * ROWS, :WIDTH]
        imag = back[i * ROWS : (i + 1) * ROWS, WIDTH:]
        turned.append(
            jnp.concatenate(
                [real * turn_cos - imag * turn_sin, imag * turn_cos + real * turn_sin], axis=0
            )
        )
    high, low = halves(jnp.concatenate(turned, axis=1))
    turned = jnp.concatenate([high, low, high], axis=0)
    last = (count - 1) * WIDTH
    values = dot(leave, turned[:, :last])
    for one in range(sequences):
        rows = slice(one * BLOCKS, (one + 1) * BLOCKS)
        columns = slice(2 * one * WIDTH, 2 * (one + 1) * WIDTH)
        out_ref[rows] = values[:, columns].astype(jnp.bfloat16)
    part_ref[...] = dot(natural, turned[:, last:])


def local_call(kernel, name, outputs, *operands):
    return pl.pallas_call(
        kernel,
        out_shape=[jax.ShapeDtypeStruct(shape, dtype) for shape, dtype in outputs],
        in_specs=[pl.BlockSpec(memory_space=pltpu.VMEM)] * len(operands),
        out_specs=[pl.BlockSpec(memory_space=pltpu.VMEM)] * len(outputs),
        compiler_params=pltpu.CompilerParams(vmem_limit_bytes=32 * 1024 * 1024),
        name=name,
    )(*operands)


def convolve(rows_in, held):
    outputs = [((rows_in.shape[0], 2 * WIDTH), jnp.bfloat16), ((BLOCKS, WIDTH), jnp.float32)]
    return local_call(convolve_kernel, "convolve", outputs, rows_in, *held)


def merge_kernel(rows_ref, part_ref, other_ref, *refs):
    count = len(refs) // 2
    out_ref = refs[count]
    total = (part_ref[...] + other_ref[...]).astype(jnp.bfloat16)
    total = dot(order(BLOCKS, runs_backward()), total).astype(jnp.bfloat16)
    out_ref[:, : 2 * WIDTH] = rows_ref[...]
    for at in range(0, rows_ref.shape[0], BLOCKS):
        out_ref[at : at + BLOCKS, 2 * WIDTH :] = total
    for source, target in zip(refs[:count], refs[count + 1 :]):
        target[...] = source[...]


def merge(rows, part, other, *arrays):
    outputs = [((rows.shape[0], 3 * WIDTH), jnp.bfloat16)]
    outputs += [(array.shape, array.dtype) for array in arrays]
    return local_call(merge_kernel, "merge", outputs, rows, part, other, *arrays)


def finish_kernel(
    rows_ref, key_ref, values_ref, grad_ref, query_out, key_out, value_out, filter_out
):
    rows = dot(order(WIDTH, runs_backward()), rows_ref[...]).astype(jnp.bfloat16)
    identity = order(WIDTH, False)
    conv_out = flip(identity, rows[:, :WIDTH])
    query_out[0] = (grad_ref[0].astype(jnp.float32) * conv_out).astype(jnp.bfloat16)
    grad_mixed = flip(identity, rows[:, WIDTH : 2 * WIDTH])
    key_out[0] = (grad_mixed * values_ref[0].astype(jnp.float32)).astype(jnp.bfloat16)
    value_out[0] = (grad_mixed * key_ref[0].astype(jnp.float32)).astype(jnp.bfloat16)
    filter_out[...] = flip(identity, rows[:, 2 * WIDTH :])


def finish(rows, *arrays):
    outputs = [(array.shape, jnp.bfloat16) for array in arrays] + [((WIDTH, WIDTH), jnp.float32)]
    return local_call(finish_kernel, "finish", outputs, rows, *arrays)


def order(size, backward):
    row = lax.broadcasted_iota(jnp.int32, (size, size), 0)
    column = lax.broadcasted_iota(jnp.int32, (size, size), 1)
    match = jnp.where(backward, size - 1 - row, row) == column
    return jnp.where(match, 1.0, 0.0).astype(jnp.bfloat16)


def flip(matrix, array):
    return lax.dot_general(
        matrix, array, (((1,), (1,)), ((), ())), preferred_element_type=jnp.float32
    )


def runs_backward():
    return lax.axis_index(CORE) == 1


def pack_kernel(mixed_ref, gated_ref, filter_ref, coarse_ref, fine_ref, packed_ref, *held_refs):
    held_coarse_ref, held_fine_ref = held_refs
    members = order(WIDTH, runs_backward())
    for at, part_ref in enumerate((mixed_ref, gated_ref, filter_ref)):
        turned = flip(members, part_ref[...])
        packed_ref[:, at * WIDTH : (at + 1) * WIDTH] = turned.astype(jnp.bfloat16)
    half = WIDTH // 2
    odd = lax.broadcasted_iota(jnp.int32, (half, WIDTH), 1) % 2 == 1
    for i in range(4):
        rows = coarse_ref[i * half : (i + 1) * half].astype(jnp.float32)
        both = jnp.concatenate([rows, jnp.where(odd, -rows, rows)], axis=0)
        held_coarse_ref[i * WIDTH : (i + 1) * WIDTH] = both.astype(jnp.bfloat16)
    held_coarse_ref[4 * WIDTH :] = coarse_ref[4 * half :]
    held_fine_ref[...] = fine_ref[...]


def pack(mixed_in, gated_grad, long_filter):
    coarse, fine = (jnp.asarray(t) for t in tables())
    packed, *held = pl.pallas_call(
        pack_kernel,
        out_shape=[
            jax.ShapeDtypeStruct((WIDTH, 3 * WIDTH), jnp.bfloat16),
            jax.ShapeDtypeStruct((coarse.shape[0] + 2 * WIDTH, WIDTH), jnp.bfloat16),
            jax.ShapeDtypeStruct(fine.shape, jnp.float32),
        ],
        in_specs=[pl.BlockSpec(memory_space=pltpu.VMEM)] * 5,
        out_specs=[pl.BlockSpec(memory_space=pltpu.VMEM)] * 3,
        compiler_params=pltpu.CompilerParams(vmem_limit_bytes=32 * 1024 * 1024),
        name="pack",
    )(mixed_in, gated_grad, long_filter, coarse, fine)
    return packed, held


def member_lists():
    places = np.arange(math.prod(SIZES)).reshape(SIZES)
    return [places[:, 0].reshape(-1).tolist(), places[:, 1].reshape(-1)[::-1].tolist()]


def exchange(rows):
    count, width = rows.shape
    moved = lax.all_to_all(
        rows.reshape(count, 2, width // 2),
        AXES,
        split_axis=0,
        concat_axis=0,
        tiled=True,
        axis_index_groups=member_lists(),
    )
    return moved.reshape(count, width)


def body(query_gate, key_gate, values_in, grad_out, long_filter):
    mixed_in = (key_gate[0].astype(jnp.float32) * values_in[0].astype(jnp.float32)).astype(
        jnp.bfloat16
    )
    gated_grad = (grad_out[0].astype(jnp.float32) * query_gate[0].astype(jnp.float32)).astype(
        jnp.bfloat16
    )
    packed, held = pack(mixed_in, gated_grad, long_filter)
    result, part = convolve(exchange(packed), held)
    other = lax.ppermute(part, CORE, [(0, 1), (1, 0)])
    merged, *arrays = merge(result, part, other, key_gate, values_in, grad_out)
    return tuple(finish(exchange(merged), *arrays))


def solution(mesh):
    fine = Mesh(mesh.devices.reshape(SIZES), (HI, CORE, LO, Y, X))
    whole = P((HI, CORE), SEQ_AXES, None)
    return jax.shard_map(
        body,
        mesh=fine,
        in_specs=(whole, whole, whole, whole, P(SEQ_AXES, None)),
        out_specs=(whole, whole, whole, P(SEQ_AXES, None)),
        check_vma=False,
    )
```

```python
import math

import jax
import jax.numpy as jnp
import numpy as np
from jax import lax
from jax.experimental import pallas as pl
from jax.experimental.pallas import tpu as pltpu
from jax.sharding import Mesh, PartitionSpec as P

HI, CORE, LO, Y, X = "hi", "core", "lo", "y", "x"
SIZES = (4, 2, 2, 8, 4)
SEQ_AXES = (LO, Y, X)
AXES = (HI, CORE, LO, Y, X)
BLOCKS = 64
WIDTH = 256
ROWS = 64
LENGTH = 2 * BLOCKS * WIDTH


def split_bf16(array):
    high = array.astype(jnp.bfloat16)
    low = (array - high.astype(np.float32)).astype(jnp.bfloat16)
    return high, low


def tables():
    freq = np.arange(ROWS)[:, None] + 0.5
    block = np.arange(BLOCKS)[None, :]
    place = np.arange(WIDTH)
    angle = 2.0 * math.pi * freq * block / (2 * BLOCKS)
    enter = np.concatenate([np.cos(angle), -np.sin(angle)], axis=0).astype(np.float32)
    scale = 2.0 / LENGTH / math.sqrt(BLOCKS * WIDTH)
    leave = (scale * np.concatenate([np.cos(angle.T), -np.sin(angle.T)], axis=1)).astype(np.float32)
    turn = 2.0 * math.pi * freq * place[None, :] / LENGTH
    angle = 2.0 * math.pi * (place[:, None] * place[None, :] % WIDTH) / WIDTH
    cos_high, cos_low = split_bf16(np.cos(angle).astype(np.float32))
    sin_high, sin_low = split_bf16(np.sin(angle).astype(np.float32))
    forward, backward = enter, enter[:, ::-1]
    coarse = np.concatenate(
        [
            cos_high[: WIDTH // 2],
            cos_low[: WIDTH // 2],
            sin_high[: WIDTH // 2],
            sin_low[: WIDTH // 2],
            np.concatenate(split_bf16(forward) + split_bf16(backward), axis=1),
            np.concatenate(split_bf16(leave), axis=1),
            np.concatenate(split_bf16(leave[::-1]), axis=1),
        ],
        axis=0,
    )
    fine = np.concatenate([np.cos(turn), np.sin(turn)], axis=0).astype(np.float32)
    return coarse, fine


def dot(left, right):
    return jnp.dot(left, right, preferred_element_type=jnp.float32)


def halves(array):
    high = array.astype(jnp.bfloat16)
    return high, (array - high.astype(jnp.float32)).astype(jnp.bfloat16)


def turn_by(parts, high_table, low_table):
    high, low = halves(parts)
    return dot(
        jnp.concatenate([high, low, high], axis=1),
        jnp.concatenate([high_table, high_table, low_table], axis=0),
    )


def complex_table(cosine, sine):
    return jnp.concatenate(
        [jnp.concatenate([cosine, sine], axis=1), jnp.concatenate([-sine, cosine], axis=1)], axis=0
    )


def convolve_kernel(x_ref, coarse_ref, fine_ref, out_ref, part_ref):
    cos_high, cos_low, sin_high, sin_low = (
        coarse_ref[i * WIDTH : (i + 1) * WIDTH] for i in range(4)
    )
    at = 4 * WIDTH
    backward = runs_backward()
    enter = jnp.where(
        backward,
        coarse_ref[at : at + 2 * ROWS, 2 * BLOCKS :],
        coarse_ref[at : at + 2 * ROWS, : 2 * BLOCKS],
    )
    at += 2 * ROWS
    natural = coarse_ref[at : at + BLOCKS]
    leave = jnp.where(backward, coarse_ref[at + BLOCKS : at + 2 * BLOCKS], natural)
    natural, leave = (
        jnp.concatenate([both[:, : 2 * ROWS], both[:, : 2 * ROWS], both[:, 2 * ROWS :]], axis=1)
        for both in (natural, leave)
    )
    sequences = x_ref.shape[0] // BLOCKS
    turn_cos, turn_sin = fine_ref[:ROWS], fine_ref[ROWS:]
    signals = []
    for one in range(sequences):
        rows = slice(one * BLOCKS, (one + 1) * BLOCKS)
        signals += [x_ref[rows, :WIDTH], x_ref[rows, WIDTH : 2 * WIDTH]]
    signals.append(x_ref[:BLOCKS, 2 * WIDTH :])
    count = len(signals)
    signals = jnp.concatenate(signals, axis=1)
    first = dot(enter, jnp.concatenate([signals, signals], axis=0))
    parts = []
    for i in range(count):
        real = first[:ROWS, i * WIDTH : (i + 1) * WIDTH]
        imag = first[ROWS:, i * WIDTH : (i + 1) * WIDTH]
        parts.append(
            jnp.concatenate(
                [real * turn_cos + imag * turn_sin, imag * turn_cos - real * turn_sin], axis=1
            )
        )
    spectra = turn_by(
        jnp.concatenate(parts, axis=0),
        complex_table(cos_high, -sin_high),
        complex_table(cos_low, -sin_low),
    )

    def spectrum(i):
        rows = slice(i * ROWS, (i + 1) * ROWS)
        return spectra[rows, :WIDTH], spectra[rows, WIDTH:]

    filt_real, filt_imag = spectrum(count - 1)
    parts = []
    total = None
    for one in range(sequences):
        mixed_real, mixed_imag = spectrum(2 * one)
        gated_real, gated_imag = spectrum(2 * one + 1)
        parts.append(
            jnp.concatenate(
                [
                    mixed_real * filt_real - mixed_imag * filt_imag,
                    mixed_real * filt_imag + mixed_imag * filt_real,
                ],
                axis=1,
            )
        )
        parts.append(
            jnp.concatenate(
                [
                    gated_real * filt_real + gated_imag * filt_imag,
                    gated_imag * filt_real - gated_real * filt_imag,
                ],
                axis=1,
            )
        )
        part = jnp.concatenate(
            [
                gated_real * mixed_real + gated_imag * mixed_imag,
                gated_imag * mixed_real - gated_real * mixed_imag,
            ],
            axis=1,
        )
        total = part if one == 0 else total + part
    parts.append(total)
    back = turn_by(
        jnp.concatenate(parts, axis=0),
        complex_table(cos_high, sin_high),
        complex_table(cos_low, sin_low),
    )
    turned = []
    for i in range(count):
        real = back[i * ROWS : (i + 1) * ROWS, :WIDTH]
        imag = back[i * ROWS : (i + 1) * ROWS, WIDTH:]
        turned.append(
            jnp.concatenate(
                [real * turn_cos - imag * turn_sin, imag * turn_cos + real * turn_sin], axis=0
            )
        )
    high, low = halves(jnp.concatenate(turned, axis=1))
    turned = jnp.concatenate([high, low, high], axis=0)
    last = (count - 1) * WIDTH
    values = dot(leave, turned[:, :last])
    for one in range(sequences):
        rows = slice(one * BLOCKS, (one + 1) * BLOCKS)
        columns = slice(2 * one * WIDTH, 2 * (one + 1) * WIDTH)
        out_ref[rows] = values[:, columns].astype(jnp.bfloat16)
    part_ref[...] = dot(natural, turned[:, last:])


def local_call(kernel, name, outputs, *operands):
    return pl.pallas_call(
        kernel,
        out_shape=[jax.ShapeDtypeStruct(shape, dtype) for shape, dtype in outputs],
        in_specs=[pl.BlockSpec(memory_space=pltpu.VMEM)] * len(operands),
        out_specs=[pl.BlockSpec(memory_space=pltpu.VMEM)] * len(outputs),
        compiler_params=pltpu.CompilerParams(vmem_limit_bytes=32 * 1024 * 1024),
        name=name,
    )(*operands)


def convolve(rows_in, held):
    outputs = [((rows_in.shape[0], 2 * WIDTH), jnp.bfloat16), ((BLOCKS, WIDTH), jnp.float32)]
    return local_call(convolve_kernel, "convolve", outputs, rows_in, *held)


def merge_kernel(rows_ref, part_ref, other_ref, *refs):
    count = len(refs) // 2
    out_ref = refs[count]
    total = (part_ref[...] + other_ref[...]).astype(jnp.bfloat16)
    total = dot(order(BLOCKS, runs_backward()), total).astype(jnp.bfloat16)
    out_ref[:, : 2 * WIDTH] = rows_ref[...]
    for at in range(0, rows_ref.shape[0], BLOCKS):
        out_ref[at : at + BLOCKS, 2 * WIDTH :] = total
    for source, target in zip(refs[:count], refs[count + 1 :]):
        target[...] = source[...]


def merge(rows, part, other, *arrays):
    outputs = [((rows.shape[0], 3 * WIDTH), jnp.bfloat16)]
    outputs += [(array.shape, array.dtype) for array in arrays]
    return local_call(merge_kernel, "merge", outputs, rows, part, other, *arrays)


def finish_kernel(
    rows_ref, key_ref, values_ref, grad_ref, query_out, key_out, value_out, filter_out
):
    members = order(WIDTH, runs_backward())
    conv_out = unflip(rows_ref[:, :WIDTH], members)
    query_out[0] = (grad_ref[0].astype(jnp.float32) * conv_out).astype(jnp.bfloat16)
    grad_mixed = unflip(rows_ref[:, WIDTH : 2 * WIDTH], members)
    key_out[0] = (grad_mixed * values_ref[0].astype(jnp.float32)).astype(jnp.bfloat16)
    value_out[0] = (grad_mixed * key_ref[0].astype(jnp.float32)).astype(jnp.bfloat16)
    filter_out[...] = unflip(rows_ref[:, 2 * WIDTH :], members)


def finish(rows, *arrays):
    outputs = [(array.shape, jnp.bfloat16) for array in arrays] + [((WIDTH, WIDTH), jnp.float32)]
    return local_call(finish_kernel, "finish", outputs, rows, *arrays)


def order(size, backward):
    row = lax.broadcasted_iota(jnp.int32, (size, size), 0)
    column = lax.broadcasted_iota(jnp.int32, (size, size), 1)
    match = jnp.where(backward, size - 1 - row, row) == column
    return jnp.where(match, 1.0, 0.0).astype(jnp.bfloat16)


def flip(matrix, array):
    return lax.dot_general(
        matrix, array, (((1,), (1,)), ((), ())), preferred_element_type=jnp.float32
    )


def unflip(array, matrix):
    return lax.dot_general(
        array, matrix, (((0,), (0,)), ((), ())), preferred_element_type=jnp.float32
    )


def runs_backward():
    return lax.axis_index(CORE) == 1


def pack_kernel(mixed_ref, gated_ref, filter_ref, coarse_ref, fine_ref, packed_ref, *held_refs):
    held_coarse_ref, held_fine_ref = held_refs
    members = order(WIDTH, runs_backward())
    for at, part_ref in enumerate((mixed_ref, gated_ref, filter_ref)):
        turned = flip(members, part_ref[...])
        packed_ref[:, at * WIDTH : (at + 1) * WIDTH] = turned.astype(jnp.bfloat16)
    half = WIDTH // 2
    odd = lax.broadcasted_iota(jnp.int32, (half, WIDTH), 1) % 2 == 1
    for i in range(4):
        rows = coarse_ref[i * half : (i + 1) * half].astype(jnp.float32)
        both = jnp.concatenate([rows, jnp.where(odd, -rows, rows)], axis=0)
        held_coarse_ref[i * WIDTH : (i + 1) * WIDTH] = both.astype(jnp.bfloat16)
    held_coarse_ref[4 * WIDTH :] = coarse_ref[4 * half :]
    held_fine_ref[...] = fine_ref[...]


def pack(mixed_in, gated_grad, long_filter):
    coarse, fine = (jnp.asarray(t) for t in tables())
    packed, *held = pl.pallas_call(
        pack_kernel,
        out_shape=[
            jax.ShapeDtypeStruct((WIDTH, 3 * WIDTH), jnp.bfloat16),
            jax.ShapeDtypeStruct((coarse.shape[0] + 2 * WIDTH, WIDTH), jnp.bfloat16),
            jax.ShapeDtypeStruct(fine.shape, jnp.float32),
        ],
        in_specs=[pl.BlockSpec(memory_space=pltpu.VMEM)] * 5,
        out_specs=[pl.BlockSpec(memory_space=pltpu.VMEM)] * 3,
        compiler_params=pltpu.CompilerParams(vmem_limit_bytes=32 * 1024 * 1024),
        name="pack",
    )(mixed_in, gated_grad, long_filter, coarse, fine)
    return packed, held


def member_lists():
    places = np.arange(math.prod(SIZES)).reshape(SIZES)
    return [places[:, 0].reshape(-1).tolist(), places[:, 1].reshape(-1)[::-1].tolist()]


def exchange(rows):
    count, width = rows.shape
    moved = lax.all_to_all(
        rows.reshape(count, 2, width // 2),
        AXES,
        split_axis=0,
        concat_axis=0,
        tiled=True,
        axis_index_groups=member_lists(),
    )
    return moved.reshape(count, width)


def body(query_gate, key_gate, values_in, grad_out, long_filter):
    mixed_in = (key_gate[0].astype(jnp.float32) * values_in[0].astype(jnp.float32)).astype(
        jnp.bfloat16
    )
    gated_grad = (grad_out[0].astype(jnp.float32) * query_gate[0].astype(jnp.float32)).astype(
        jnp.bfloat16
    )
    packed, held = pack(mixed_in, gated_grad, long_filter)
    result, part = convolve(exchange(packed), held)
    other = lax.ppermute(part, CORE, [(0, 1), (1, 0)])
    merged, *arrays = merge(result, part, other, key_gate, values_in, grad_out)
    return tuple(finish(exchange(merged), *arrays))


def solution(mesh):
    fine = Mesh(mesh.devices.reshape(SIZES), (HI, CORE, LO, Y, X))
    whole = P((HI, CORE), SEQ_AXES, None)
    return jax.shard_map(
        body,
        mesh=fine,
        in_specs=(whole, whole, whole, whole, P(SEQ_AXES, None)),
        out_specs=(whole, whole, whole, P(SEQ_AXES, None)),
        check_vma=False,
    )
```
